512 devices in a mesh: row: 16 (over z, x_hi), col: 32 (over y, x_lo, core).
Axes of the slice: x: 4 (x_hi: 2, x_lo: 2; x = x_hi * 2 + x_lo), y: 8, z: 8, core: 2. Of those that a mesh axis runs over, the one named last changes fastest.
Arguments:
- hamiltonian: float32 [12288, 12288], P('row', 'col'), may hold values from -40 to 40, as said below
- panel: float32 [12288, 256], P('row'), may hold values from -180 to 180
Outputs:
- updated: float32 [12288, 12288], P('row', 'col')
- band_block: float32 [256, 256], replicated
The draws below stay inside these ranges and needn't reach their ends.
Inputs may be any that keep to these rules, and one draw needn't show every extreme that they name: hamiltonian is exactly symmetric.
All inputs are finite; a program needn't handle non-finite values.
Results may differ from the reference program's by a relative error of at most 0.0003.
Values sent between devices are 32-bit elements; how exact they have to be, the bound alone decides.
A program may use at most 64 MiB of HBM per device.

```python
import jax
import jax.numpy as jnp
from jax import lax

NB = 256
ORDER = 12288


def draw_hamiltonian(key, part):
    key = jax.random.fold_in(key, 11)
    key_vals = jax.random.fold_in(key, 0)
    raw = jnp.clip(jax.random.normal(key_vals, (ORDER, ORDER), jnp.float32), -6.0, 6.0)
    return (raw + raw.T) * 0.7071


def draw_panel(key, part):
    key = jax.random.fold_in(key, 23)
    key_vals = jax.random.fold_in(key, 0)
    key_cols = jax.random.fold_in(key, 1)
    key_common = jax.random.fold_in(key, 3)
    col_scale = jnp.exp(jax.random.uniform(key_cols, (NB,), jnp.float32, 0.0, 2.302))
    raw = jnp.clip(jax.random.normal(key_vals, (ORDER, NB), jnp.float32), -6.0, 6.0)
    common = jnp.clip(jax.random.normal(key_common, (ORDER, 1), jnp.float32), -6.0, 6.0)
    return (common + 0.008 * raw) * col_scale[None, :]


def setup_inputs(seed: int = 0) -> dict:
    arg_keys = jax.random.split(jax.random.key(seed), 3)
    return {
        "hamiltonian": draw_hamiltonian(jax.random.fold_in(arg_keys[2], 71), 0),
        "panel": draw_panel(jax.random.fold_in(arg_keys[2], 71), 0),
    }


def mult(left, right):
    return jnp.dot(left.astype(jnp.float32), right.astype(jnp.float32), precision=lax.Precision.HIGHEST, preferred_element_type=jnp.float32)

def reference(hamiltonian, panel):
    first_low = jnp.linalg.cholesky(mult(panel.T, panel))
    half = jax.scipy.linalg.solve_triangular(first_low, panel.T, lower=True).T
    second_low = jnp.linalg.cholesky(mult(half.T, half))
    ortho = jax.scipy.linalg.solve_triangular(second_low, half.T, lower=True).T
    ident = jnp.eye(NB, dtype=jnp.float32)
    lead = ortho[:NB] + ident
    reflectors = jnp.concatenate([lead, ortho[NB:]], axis=0)
    factor = jnp.linalg.solve(lead.T, ident)
    products = mult(hamiltonian, reflectors)
    images = mult(products, factor)
    coupling = mult(reflectors.T, images)
    correction = images - 0.5 * mult(reflectors, mult(factor.T, coupling))
    updated = hamiltonian - mult(reflectors, correction.T) - mult(correction, reflectors.T)
    band_block = -mult(second_low.T, first_low.T)
    return (updated, band_block)
```

```python
import functools

import jax
import jax.numpy as jnp
from jax import lax
from jax.experimental import pallas as pl
from jax.experimental.pallas import tpu as pltpu
from jax.sharding import PartitionSpec as P

HI = lax.Precision.HIGHEST
MESH = pl.DeviceIdType.MESH
N = 256


def mm(a, b, ca, cb):
    return lax.dot_general(a, b, (((ca,), (cb,)), ((), ())), precision=HI, preferred_element_type=jnp.float32)

def spread(x, i, rows):
    return jnp.broadcast_to(x[i:i+1, :], (rows, 128))

def stack(parts):
    parts = [p for p in parts if p.shape[0]]
    return parts[0] if len(parts) == 1 else jnp.concatenate(parts, axis=0)

def halves(o):
    return ([0, 1] if o < 128 else [1]), ([0] if o < 128 else [0, 1])

def chol_inv(a, w, u, li, B):
    row = lax.broadcasted_iota(jnp.int32, (N, N), 0)
    col = lax.broadcasted_iota(jnp.int32, (N, N), 1)
    w[...] = jnp.where(row == col, 1.0, 0.0).astype(jnp.float32)
    sub = lax.broadcasted_iota(jnp.int32, (8, 128), 0)
    for o in range(0, N, B):
        ha, hw = halves(o)
        X = [a[o:o+B, 128*h:128*h+128] for h in ha] + [w[o:o+B, 128*h:128*h+128] for h in hw]
        for q in range(0, B, 8):
            k0 = o + q
            R = B - q
            base = X[ha.index(k0 // 128)]
            l0 = k0 % 128
            C = [jnp.broadcast_to(base[:, l0+k:l0+k+1], (R, 128)) for k in range(8)]
            scale = jnp.ones((8, 128), jnp.float32)
            for i in range(0, 8, 2):
                pa, pb, pd = C[i][i:i+1, :], C[i][i+1:i+2, :], C[i+1][i+1:i+2, :]
                pa, pb, pd = [jnp.broadcast_to(p, (8, 128)) for p in (pa, pb, pd)]
                det = pa*pd - pb*pb
                ra = 1.0 / pa
                rdet = 1.0 / det
                scale = jnp.where(sub == i, lax.rsqrt(pa), jnp.where(sub == i+1, lax.rsqrt(det*ra), scale))
                full = lambda p: jnp.concatenate([p]*(R//8), axis=0) if R > 8 else p
                fa, fb, fra, frd = full(pa), full(pb), full(ra), full(rdet)
                m2 = (C[i+1]*fa - C[i]*fb)*frd
                m1 = (C[i] - m2*fb)*fra
                m2 = stack([jnp.where(sub > i+1, m2[:8], 0.0), m2[8:]])
                m1 = stack([jnp.where(sub > i+1, m1[:8], jnp.where(sub == i+1, pb*ra, 0.0)), m1[8:]])
                for k in range(i+2, 8):
                    C[k] = (C[k] - m1*spread(C[k], i, R)) - m2*spread(C[k], i+1, R)
                X = [(x - m1*spread(x, i, R)) - m2*spread(x, i+1, R) for x in X]
            top = [x[:8]*scale for x in X]
            X = [x[8:] for x in X]
            for j, h in enumerate(ha):
                u[k0:k0+8, 128*h:128*h+128] = top[j]
            for j, h in enumerate(hw):
                li[k0:k0+8, 128*h:128*h+128] = top[len(ha)+j]
            if ha == [1]:
                u[k0:k0+8, 0:128] = jnp.zeros((8, 128), jnp.float32)
            if hw == [0]:
                li[k0:k0+8, 128:256] = jnp.zeros((8, 128), jnp.float32)
        e = o + B
        if e < N:
            a0 = 128 * (e // 128)
            lw = 128 if e <= 128 else 256
            for (m0, m1) in ((e, e+B), (e+B, N)):
                if m0 >= m1: continue
                lhs = u[o:e, :][:, m0:m1]
                a[m0:m1, a0:N] -= mm(lhs, u[o:e, a0:N], 0, 0)
                w[m0:m1, 0:lw] -= mm(lhs, li[o:e, 0:lw], 0, 0)
    u[...] = jnp.where(row <= col, u[...], 0.0)

def gj_init(w):
    row = lax.broadcasted_iota(jnp.int32, (N, N), 0)
    col = lax.broadcasted_iota(jnp.int32, (N, N), 1)
    w[...] = jnp.where(row == col, 1.0, 0.0).astype(jnp.float32)

def gj_inv(a, w, o, B):
    sub = lax.broadcasted_iota(jnp.int32, (8, 128), 0)
    ha, hw = halves(o)
    X = [a[o:o+B, 128*h:128*h+128] for h in ha] + [w[o:o+B, 128*h:128*h+128] for h in hw]
    scales = []
    for q in range(0, B, 8):
        k0 = o + q
        base = X[ha.index(k0 // 128)]
        l0 = k0 % 128
        C = [jnp.broadcast_to(base[:, l0+k:l0+k+1], (B, 128)) for k in range(8)]
        scale = jnp.ones((8, 128), jnp.float32)
        for i in range(8):
            p = jnp.broadcast_to(C[i][q+i:q+i+1, :], (8, 128))
            r = 1.0 / p
            scale = jnp.where(sub == i, r, scale)
            m = C[i] * (jnp.concatenate([r]*(B//8), axis=0) if B > 8 else r)
            m = stack([m[:q], jnp.where(sub == i, 0.0, m[q:q+8]), m[q+8:]])
            for k in range(i+1, 8):
                C[k] = C[k] - m*spread(C[k], q+i, B)
            X = [x - m*spread(x, q+i, B) for x in X]
        scales.append(scale)
    scale = jnp.concatenate(scales, axis=0)
    X = [x*scale for x in X]
    for j, h in enumerate(ha):
        a[o:o+B, 128*h:128*h+128] = X[j]
    for j, h in enumerate(hw):
        w[o:o+B, 128*h:128*h+128] = X[len(ha)+j]
    e = o + B
    a0 = 128 * (e // 128)
    lw = 128 if e <= 128 else 256
    h = o // 128
    for (m0, m1) in ((0, o), (e, N)):
        if m0 >= m1: continue
        lhs = a[m0:m1, 128*h:128*h+128][:, o-128*h:e-128*h]
        if a0 < N:
            a[m0:m1, a0:N] -= mm(lhs, a[o:e, a0:N], 1, 0)
        w[m0:m1, 0:lw] -= mm(lhs, w[o:e, 0:lw], 1, 0)

def kernel(p_ref, h_any, out_ref, band_ref, hbuf, gp1, gp2, rs1, rs2, red1, red2, g1, g2, pts, pt, pc,
           half, vr, vc, a, w, u1, l1, u2, l2, mbuf, mrecv, obuf, cbuf, crs, rrs, hvr, hvc,
           sbuf, srs, s1, smate, scx, sfull,
           h_sem, send, recv, mate_send, mate_recv):
    r = lax.axis_index("row")
    c = lax.axis_index("col")
    core = lax.rem(c, 2)
    chip = lax.div(c, 2)
    mate = (r, c + 1 - 2 * core)
    other = 1 - core
    RW, CW = 16, 16

    def rcopy(src, dst, ph, slot, dst_slot, dev):
        return pltpu.make_async_remote_copy(src_ref=src, dst_ref=dst, send_sem=send.at[ph, slot],
                                            recv_sem=recv.at[ph, dst_slot], device_id=dev, device_id_type=MESH)

    def mcopy(src, dst, ph, slot):
        return pltpu.make_async_remote_copy(src_ref=src, dst_ref=dst, send_sem=mate_send.at[ph, slot],
                                            recv_sem=mate_recv.at[ph, slot], device_id=mate, device_id_type=MESH)

    def row_dev(k):
        return (k, c)

    def col_dev(k):
        return (r, 2 * k + core)

    def spread_send(ph, me, dev, src, dst):
        def step(d, x):
            k = lax.rem(me + d, 16)
            rcopy(src(k), dst(me), ph, k, me, dev(k)).start()
            return x
        lax.fori_loop(1, 16, step, 0)

    def spread_recv(ph, me, dev, src, dst, then=None):
        def step(d, x):
            k = lax.rem(me + 16 - d, 16)
            rcopy(src(k), dst(k), ph, k, k, dev(k)).wait_recv()
            if then is not None:
                then(k)
            return x
        lax.fori_loop(1, 16, step, 0)

    def spread_done(ph, me, dev, src, dst):
        def step(d, x):
            k = lax.rem(me + d, 16)
            rcopy(src(k), dst(me), ph, k, me, dev(k)).wait_send()
            return x
        lax.fori_loop(1, 16, step, 0)

    h_copy = pltpu.make_async_copy(h_any, hbuf, h_sem)
    h_copy.start()

    barrier = pltpu.get_barrier_semaphore()

    def greet(d, x):
        pl.semaphore_signal(barrier, inc=1, device_id=row_dev(lax.rem(r + d, 16)), device_id_type=MESH)
        pl.semaphore_signal(barrier, inc=1, device_id=col_dev(lax.rem(chip + d, 16)), device_id_type=MESH)
        return x
    lax.fori_loop(1, 16, greet, 0)
    pl.semaphore_signal(barrier, inc=1, device_id=mate, device_id_type=MESH)
    diag = chip == r

    def greet_pc(j, x):
        @pl.when(jnp.logical_not(jnp.logical_and(diag, j == r)))
        def _():
            pl.semaphore_signal(barrier, inc=1, device_id=(chip, 2 * j + core), device_id_type=MESH)
        return x
    lax.fori_loop(0, 16, greet_pc, 0)

    my_cols = pl.ds(pl.multiple_of(core * 128, 128), 128)

    def gram(x_ref, gp):
        gp[...] = mm(x_ref[...], x_ref[:, my_cols], 0, 0)

    gram(p_ref, gp1)
    pl.semaphore_wait(barrier, 47 - diag.astype(jnp.int32))

    def rows16(ref, k):
        return ref.at[pl.ds(pl.multiple_of(k * 16, 16), 16), :]

    def allreduce(ph, gp, rs, red, g):
        src, dst = (lambda k: rows16(gp, k)), (lambda k: rs.at[k])
        spread_send(ph, r, row_dev, src, dst)
        rs[r] = rows16(gp, r)[...]
        spread_recv(ph, r, row_dev, src, dst)
        total = rs[0]
        for k in range(1, 16):
            total = total + rs[k]
        red[...] = total
        mine = g.at[core]
        gsrc, gdst = (lambda k: red), (lambda k: rows16(mine, k))
        spread_send(ph + 1, r, row_dev, gsrc, gdst)
        rows16(mine, r)[...] = total
        return gsrc, gdst

    def share_mine(ph, ref):
        mcopy(rows16(ref.at[core], r), rows16(ref.at[core], r), ph, r).start()

    def finish_gather(ph, mph, g, gsrc, gdst):
        mine = g.at[core]

        def forward(k):
            mcopy(rows16(mine, k), rows16(mine, k), mph, k).start()
        forward(r)
        spread_recv(ph, r, row_dev, gsrc, gdst, forward)

        def step(k, x):
            mcopy(rows16(mine, k), rows16(g.at[other], k), mph, k).wait_recv()
            return x
        lax.fori_loop(0, 16, step, 0)

    tsrc, tdst = (lambda k: p_ref.at[pl.ds(pl.multiple_of(k * 16, 16), 16), my_cols]), (lambda k: pts)

    gsrc, gdst = allreduce(0, gp1, rs1, red1, g1)

    @pl.when(r == 0)
    def _():
        def step(k, x):
            rcopy(tsrc(k), pts, 2, k, 0, row_dev(k)).start()
            return x
        lax.fori_loop(1, 16, step, 0)
        pts[...] = tsrc(0)[...]

    slab = pl.ds(pl.multiple_of(core * 384 + chip * 24, 8), 24)

    def pc_rows(j):
        return pc.at[pl.ds(pl.multiple_of(j * 24, 8), 24), :]

    def pc_send(d, x):
        k = lax.rem(r + d, 16)

        @pl.when(jnp.logical_and(diag, k == r))
        def _():
            pc_rows(chip)[...] = p_ref[slab, :]

        @pl.when(jnp.logical_not(jnp.logical_and(diag, k == r)))
        def _():
            rcopy(p_ref.at[slab, :], pc_rows(chip), 4, k, chip, (k, 2 * r + core)).start()
        return x
    lax.fori_loop(0, 16, pc_send, 0)

    finish_gather(1, 0, g1, gsrc, gdst)
    a[:, 0:128] = g1[0]
    a[:, 128:256] = g1[1]

    @pl.when(r != 0)
    def _():
        rcopy(pts, pts, 2, 0, 0, row_dev(0)).wait_recv()
    tmine = pt.at[core]
    t2src, t2dst = (lambda k: pts), (lambda k: rows16(tmine, k))
    spread_send(3, r, row_dev, t2src, t2dst)
    rows16(tmine, r)[...] = pts[...]

    chol_inv(a, w, u1, l1, 64)

    half[...] = mm(p_ref[...], l1[...], 1, 1)
    gram(half, gp2)
    gsrc2, gdst2 = allreduce(5, gp2, rs2, red2, g2)
    finish_gather(3, 1, pt, t2src, t2dst)

    def pc_recv(j, x):
        @pl.when(jnp.logical_not(jnp.logical_and(diag, j == r)))
        def _():
            rcopy(p_ref.at[slab, :], pc_rows(j), 4, 0, j, (chip, 2 * j + core)).wait_recv()
        return x
    lax.fori_loop(0, 16, pc_recv, 0)
    vc[...] = mm(pc[...], l1[...], 1, 1)
    finish_gather(6, 2, g2, gsrc2, gdst2)
    a[:, 0:128] = g2[0]
    a[:, 128:256] = g2[1]
    chol_inv(a, w, u2, l2, 64)

    grow = lax.broadcasted_iota(jnp.int32, (N, N), 0)
    gcol = lax.broadcasted_iota(jnp.int32, (N, N), 1)
    ident = jnp.where(grow == gcol, 1.0, 0.0).astype(jnp.float32)
    vr[...] = mm(half[...], l2[...], 1, 1)
    vc[...] = mm(vc[...], l2[...], 1, 1)

    @pl.when(r == 0)
    def _():
        vr[0:N, :] += ident

    @pl.when(c == 0)
    def _():
        vc[0:N, :] += ident
    h_copy.wait()

    theirs = pl.multiple_of(other * 384, 384)
    ours = pl.multiple_of(core * 384, 384)

    def mate_rows(ref, q):
        return ref.at[96 * q:96 * q + 96, :]
    for q in range(4):
        mbuf[96 * q:96 * q + 96, :] = mm(hbuf[pl.ds(theirs + 96 * q, 96), :], vc[...], 1, 0)
        mcopy(mate_rows(mbuf, q), mate_rows(mrecv, q), 3, q).start()
    cbuf[...] = mm(hbuf[...], vr[...], 0, 0)

    def rows24(ref, k):
        return ref.at[pl.ds(pl.multiple_of(k * 24, 8), 24), :]
    rsrc, rdst = (lambda k: rows24(cbuf, k)), (lambda k: rrs.at[k])
    spread_send(7, r, row_dev, rsrc, rdst)
    rrs[r] = rows24(cbuf, r)[...]
    obuf[...] = mm(hbuf[pl.ds(ours, 384), :], vc[...], 1, 0)
    csrc, cdst = (lambda k: rows24(obuf, k)), (lambda k: crs.at[k])
    for q in range(4):
        mcopy(mate_rows(mbuf, q), mate_rows(mrecv, q), 3, q).wait_recv()
        obuf[96 * q:96 * q + 96, :] += mrecv[96 * q:96 * q + 96, :]
    spread_send(8, chip, col_dev, csrc, cdst)
    crs[chip] = rows24(obuf, chip)[...]
    sbuf[...] = mm(vr[pl.ds(ours, 384), :], obuf[...], 0, 0)
    ssrc, sdst = (lambda k: rows16(sbuf, k)), (lambda k: srs.at[k])
    spread_send(9, r, row_dev, ssrc, sdst)
    srs[r] = rows16(sbuf, r)[...]

    a[:, :] = mm(jnp.concatenate([pt[0], pt[1]], axis=1), l1[...], 1, 1)
    a[...] = mm(a[...], l2[...], 1, 1) + ident
    gj_init(w)
    gj_inv(a, w, 0, 32)
    gj_inv(a, w, 32, 32)

    spread_recv(9, r, row_dev, ssrc, sdst)
    total = srs[0]
    for k in range(1, 16):
        total = total + srs[k]
    s1[...] = total

    def rows8(ref, k):
        return ref.at[pl.ds(pl.multiple_of(k * 8, 8), 8), :]
    mcopy(rows8(s1, other), smate, 4, 0).start()
    gj_inv(a, w, 64, 32)
    mcopy(rows8(s1, other), smate, 4, 0).wait_recv()
    s2 = scx.at[chip]
    s2[...] = rows8(s1, core)[...] + smate[...]
    xsrc, xdst = (lambda k: scx.at[chip]), (lambda k: scx.at[k])
    spread_send(10, chip, col_dev, xsrc, xdst)
    gj_inv(a, w, 96, 32)

    spread_recv(7, r, row_dev, rsrc, rdst)
    total = rrs[0]
    for k in range(1, 16):
        total = total + rrs[k]
    rows24(hvc, r)[...] = total
    bsrc, bdst = (lambda k: rows24(hvc, r)), (lambda k: rows24(hvc, k))
    spread_send(11, r, row_dev, bsrc, bdst)

    def rows_own(k):
        return hvr.at[pl.ds(pl.multiple_of(ours + k * 24, 8), 24), :]

    def rows_their(k):
        return hvr.at[pl.ds(pl.multiple_of(theirs + k * 24, 8), 24), :]
    spread_recv(8, chip, col_dev, csrc, cdst)
    total = crs[0]
    for k in range(1, 16):
        total = total + crs[k]
    rows_own(chip)[...] = total
    asrc, adst = (lambda k: rows_own(chip)), rows_own
    spread_send(12, chip, col_dev, asrc, adst)

    def forward(k):
        mcopy(rows_own(k), rows_own(k), 5, k).start()
    forward(chip)
    gj_inv(a, w, 128, 32)

    spread_recv(10, chip, col_dev, xsrc, xdst)
    total = scx[0]
    for k in range(1, 16):
        total = total + scx[k]

    def srow(k, half_of):
        return sfull.at[pl.ds(pl.multiple_of(k * 16 + half_of * 8, 8), 8), :]
    srow(r, core)[...] = total
    fsrc, fdst = (lambda k: srow(r, core)), (lambda k: srow(k, core))
    spread_send(13, r, row_dev, fsrc, fdst)

    def s_forward(k):
        mcopy(srow(k, core), srow(k, core), 6, k).start()
    s_forward(r)
    gj_inv(a, w, 160, 32)
    gj_inv(a, w, 192, 32)
    gj_inv(a, w, 224, 32)
    spread_recv(13, r, row_dev, fsrc, fdst, s_forward)
    vr[...] = mm(vr[...], w[...], 1, 0)
    vc[...] = mm(vc[...], w[...], 1, 0)

    def s_mate(k, x):
        mcopy(srow(k, core), srow(k, other), 6, k).wait_recv()
        return x
    lax.fori_loop(0, 16, s_mate, 0)
    spread_recv(12, chip, col_dev, asrc, adst, forward)
    sv = mm(sfull[...], vc[...], 1, 1)
    hbuf[...] += mm(vr[...], sv, 1, 0)
    spread_recv(11, r, row_dev, bsrc, bdst)
    hbuf[...] -= mm(vr[...], hvc[...], 1, 1)

    def hv_mate(k, x):
        mcopy(rows_own(k), rows_their(k), 5, k).wait_recv()
        return x
    lax.fori_loop(0, 16, hv_mate, 0)
    out_ref[...] = hbuf[...] - mm(hvr[...], vc[...], 1, 1)
    band_ref[...] = -mm(u2[...], u1[...], 1, 0)

    spread_done(0, r, row_dev, lambda k: rows16(gp1, k), lambda k: rs1.at[k])
    spread_done(1, r, row_dev, gsrc, gdst)

    @pl.when(r == 0)
    def _():
        def step(k, x):
            rcopy(tsrc(k), pts, 2, k, 0, row_dev(k)).wait_send()
            return x
        lax.fori_loop(1, 16, step, 0)
    spread_done(3, r, row_dev, t2src, t2dst)

    def pc_done(k, x):
        @pl.when(jnp.logical_not(jnp.logical_and(diag, k == r)))
        def _():
            rcopy(p_ref.at[slab, :], pc_rows(chip), 4, k, chip, (k, 2 * r + core)).wait_send()
        return x
    lax.fori_loop(0, 16, pc_done, 0)
    spread_done(5, r, row_dev, lambda k: rows16(gp2, k), lambda k: rs2.at[k])
    spread_done(6, r, row_dev, gsrc2, gdst2)
    spread_done(7, r, row_dev, rsrc, rdst)
    spread_done(8, chip, col_dev, csrc, cdst)
    spread_done(9, r, row_dev, ssrc, sdst)
    spread_done(10, chip, col_dev, xsrc, xdst)
    spread_done(11, r, row_dev, bsrc, bdst)
    spread_done(12, chip, col_dev, asrc, adst)
    spread_done(13, r, row_dev, fsrc, fdst)

    def mates_done(k, x):
        mcopy(rows16(g1.at[core], k), rows16(g1.at[core], k), 0, k).wait_send()
        mcopy(rows16(pt.at[core], k), rows16(pt.at[core], k), 1, k).wait_send()
        mcopy(rows16(g2.at[core], k), rows16(g2.at[core], k), 2, k).wait_send()
        mcopy(rows_own(k), rows_own(k), 5, k).wait_send()
        mcopy(srow(k, core), srow(k, core), 6, k).wait_send()
        return x
    lax.fori_loop(0, 16, mates_done, 0)
    for q in range(4):
        mcopy(mate_rows(mbuf, q), mate_rows(mrecv, q), 3, q).wait_send()
    mcopy(rows8(s1, other), smate, 4, 0).wait_send()


def shards(hamiltonian, panel):
    vm = pl.BlockSpec(memory_space=pltpu.VMEM)
    f32 = lambda *s: pltpu.VMEM(s, jnp.float32)
    sq = f32(N, N)
    scratch = [f32(768, 384), f32(N, 128), f32(N, 128), f32(16, 16, 128), f32(16, 16, 128),
               f32(16, 128), f32(16, 128), f32(2, N, 128), f32(2, N, 128), f32(16, 128), f32(2, N, 128),
               f32(384, N), f32(768, N), f32(768, N), f32(384, N), sq, sq, sq, sq, sq, sq,
               f32(384, N), f32(384, N), f32(384, N), f32(384, N), f32(16, 24, N), f32(16, 24, N),
               f32(768, N), f32(384, N), sq, f32(16, 16, N), f32(16, N), f32(8, N), f32(16, 8, N), sq,
               pltpu.SemaphoreType.DMA, pltpu.SemaphoreType.DMA((14, 16)), pltpu.SemaphoreType.DMA((14, 16)),
               pltpu.SemaphoreType.DMA((7, 16)), pltpu.SemaphoreType.DMA((7, 16))]
    return pl.pallas_call(
        kernel,
        out_shape=[jax.ShapeDtypeStruct((768, 384), jnp.float32), jax.ShapeDtypeStruct((N, N), jnp.float32)],
        in_specs=[vm, pl.BlockSpec(memory_space=pl.ANY)],
        out_specs=[vm, vm],
        scratch_shapes=scratch,
        compiler_params=pltpu.CompilerParams(collective_id=0, has_side_effects=True, vmem_limit_bytes=48 * 2**20),
        cost_estimate=pl.CostEstimate(flops=3 * 10**9, bytes_accessed=4 * 10**6, transcendentals=0),
    )(panel, hamiltonian)


def solution(mesh):
    in_specs = (P("row", "col"), P("row", None))
    out_specs = (P("row", "col"), P())
    return jax.shard_map(shards, mesh=mesh, in_specs=in_specs, out_specs=out_specs, check_vma=False)
```

```python
import functools

import jax
import jax.numpy as jnp
from jax import lax
from jax.experimental import pallas as pl
from jax.experimental.pallas import tpu as pltpu
from jax.sharding import PartitionSpec as P

HI = lax.Precision.HIGHEST
MESH = pl.DeviceIdType.MESH
N = 256


def mm(a, b, ca, cb):
    return lax.dot_general(a, b, (((ca,), (cb,)), ((), ())), precision=HI, preferred_element_type=jnp.float32)

def spread(x, i, rows):
    return jnp.broadcast_to(x[i:i+1, :], (rows, 128))

def stack(parts):
    parts = [p for p in parts if p.shape[0]]
    return parts[0] if len(parts) == 1 else jnp.concatenate(parts, axis=0)

def halves(o):
    return ([0, 1] if o < 128 else [1]), ([0] if o < 128 else [0, 1])

def chol_inv(a, w, u, li, B):
    row = lax.broadcasted_iota(jnp.int32, (N, N), 0)
    col = lax.broadcasted_iota(jnp.int32, (N, N), 1)
    w[...] = jnp.where(row == col, 1.0, 0.0).astype(jnp.float32)
    sub = lax.broadcasted_iota(jnp.int32, (8, 128), 0)
    for o in range(0, N, B):
        ha, hw = halves(o)
        X = [a[o:o+B, 128*h:128*h+128] for h in ha] + [w[o:o+B, 128*h:128*h+128] for h in hw]
        for q in range(0, B, 8):
            k0 = o + q
            R = B - q
            base = X[ha.index(k0 // 128)]
            l0 = k0 % 128
            C = [jnp.broadcast_to(base[:, l0+k:l0+k+1], (R, 128)) for k in range(8)]
            scale = jnp.ones((8, 128), jnp.float32)
            for i in range(0, 8, 2):
                pa, pb, pd = C[i][i:i+1, :], C[i][i+1:i+2, :], C[i+1][i+1:i+2, :]
                pa, pb, pd = [jnp.broadcast_to(p, (8, 128)) for p in (pa, pb, pd)]
                det = pa*pd - pb*pb
                ra = 1.0 / pa
                rdet = 1.0 / det
                scale = jnp.where(sub == i, lax.rsqrt(pa), jnp.where(sub == i+1, lax.rsqrt(det*ra), scale))
                full = lambda p: jnp.concatenate([p]*(R//8), axis=0) if R > 8 else p
                fa, fb, fra, frd = full(pa), full(pb), full(ra), full(rdet)
                m2 = (C[i+1]*fa - C[i]*fb)*frd
                m1 = (C[i] - m2*fb)*fra
                m2 = stack([jnp.where(sub > i+1, m2[:8], 0.0), m2[8:]])
                m1 = stack([jnp.where(sub > i+1, m1[:8], jnp.where(sub == i+1, pb*ra, 0.0)), m1[8:]])
                for k in range(i+2, 8):
                    C[k] = (C[k] - m1*spread(C[k], i, R)) - m2*spread(C[k], i+1, R)
                X = [(x - m1*spread(x, i, R)) - m2*spread(x, i+1, R) for x in X]
            top = [x[:8]*scale for x in X]
            X = [x[8:] for x in X]
            for j, h in enumerate(ha):
                u[k0:k0+8, 128*h:128*h+128] = top[j]
            for j, h in enumerate(hw):
                li[k0:k0+8, 128*h:128*h+128] = top[len(ha)+j]
            if ha == [1]:
                u[k0:k0+8, 0:128] = jnp.zeros((8, 128), jnp.float32)
            if hw == [0]:
                li[k0:k0+8, 128:256] = jnp.zeros((8, 128), jnp.float32)
        e = o + B
        if e < N:
            a0 = 128 * (e // 128)
            lw = 128 if e <= 128 else 256
            for (m0, m1) in ((e, e+B), (e+B, N)):
                if m0 >= m1: continue
                lhs = u[o:e, :][:, m0:m1]
                a[m0:m1, a0:N] -= mm(lhs, u[o:e, a0:N], 0, 0)
                w[m0:m1, 0:lw] -= mm(lhs, li[o:e, 0:lw], 0, 0)
    u[...] = jnp.where(row <= col, u[...], 0.0)

def gj_init(w):
    row = lax.broadcasted_iota(jnp.int32, (N, N), 0)
    col = lax.broadcasted_iota(jnp.int32, (N, N), 1)
    w[...] = jnp.where(row == col, 1.0, 0.0).astype(jnp.float32)

def gj_inv(a, w, o, B):
    sub = lax.broadcasted_iota(jnp.int32, (8, 128), 0)
    ha, hw = halves(o)
    X = [a[o:o+B, 128*h:128*h+128] for h in ha] + [w[o:o+B, 128*h:128*h+128] for h in hw]
    scales = []
    for q in range(0, B, 8):
        k0 = o + q
        base = X[ha.index(k0 // 128)]
        l0 = k0 % 128
        C = [jnp.broadcast_to(base[:, l0+k:l0+k+1], (B, 128)) for k in range(8)]
        scale = jnp.ones((8, 128), jnp.float32)
        for i in range(8):
            p = jnp.broadcast_to(C[i][q+i:q+i+1, :], (8, 128))
            r = 1.0 / p
            scale = jnp.where(sub == i, r, scale)
            m = C[i] * (jnp.concatenate([r]*(B//8), axis=0) if B > 8 else r)
            m = stack([m[:q], jnp.where(sub == i, 0.0, m[q:q+8]), m[q+8:]])
            for k in range(i+1, 8):
                C[k] = C[k] - m*spread(C[k], q+i, B)
            X = [x - m*spread(x, q+i, B) for x in X]
        scales.append(scale)
    scale = jnp.concatenate(scales, axis=0)
    X = [x*scale for x in X]
    for j, h in enumerate(ha):
        a[o:o+B, 128*h:128*h+128] = X[j]
    for j, h in enumerate(hw):
        w[o:o+B, 128*h:128*h+128] = X[len(ha)+j]
    e = o + B
    a0 = 128 * (e // 128)
    lw = 128 if e <= 128 else 256
    h = o // 128
    for (m0, m1) in ((0, o), (e, N)):
        if m0 >= m1: continue
        lhs = a[m0:m1, 128*h:128*h+128][:, o-128*h:e-128*h]
        if a0 < N:
            a[m0:m1, a0:N] -= mm(lhs, a[o:e, a0:N], 1, 0)
        w[m0:m1, 0:lw] -= mm(lhs, w[o:e, 0:lw], 1, 0)

PHASES = ("g1", "g1c", "tr", "top", "pc", "topg", "g2", "g2c", "s", "sx", "sg", "hr", "hc", "hrg", "hcg",
          "m_g1", "m_g2", "m_top", "m_h0", "m_h1", "m_s", "m_sg", "m_hg")


def kernel(p_any, h_any, out_ref, band_ref, p_ref, hbuf, gp, ex1, ex2, g1, g2, pts, pt, pcs, pc,
           half, vr, vc, a, w, u1, l1, u2, l2, mbuf, mrecv, obuf, cbuf, crs, rrs, hvr, hvc,
           sbuf, srs, s1, smate, scx, sfull, p_sem, h_sem, send, recv):
    r = lax.axis_index("row")
    c = lax.axis_index("col")
    core = lax.rem(c, 2)
    chip = lax.div(c, 2)
    other = 1 - core
    mate = (r, 2 * chip + other)
    turned = (chip, 2 * r + core)
    diag = chip == r
    done = []

    def rcopy(src, dst, name, dev):
        i = PHASES.index(name)
        return pltpu.make_async_remote_copy(src_ref=src, dst_ref=dst, send_sem=send.at[i], recv_sem=recv.at[i],
                                            device_id=dev, device_id_type=MESH)

    def one(src, dst, name, dev):
        rcopy(src, dst, name, dev).start()
        done.append(lambda: rcopy(src, dst, name, dev).wait_send())

    def got(dst, name):
        rcopy(dst, dst, name, mate).wait_recv()

    def row_dev(k):
        return (k, c)

    def col_dev(k):
        return (r, 2 * k + core)

    def spread(name, me, dev, src, dst, fifteen):
        def step(d, x):
            k = lax.rem(me + d, 16)
            rcopy(src(k), dst, name, dev(k)).start()
            return x
        lax.fori_loop(1, 16, step, 0)
        done.append(lambda: rcopy(fifteen, fifteen, name, mate).wait_send())

    def rows(ref, k, n):
        return ref.at[pl.ds(pl.multiple_of(k * n, 8), n), :]

    def total(ref):
        t = ref[0]
        for k in range(1, 16):
            t = t + ref[k]
        return t

    p_copy = pltpu.make_async_copy(p_any, p_ref, p_sem)
    p_copy.start()
    h_copy = pltpu.make_async_copy(h_any, hbuf, h_sem)
    h_copy.start()

    barrier = pltpu.get_barrier_semaphore()

    def greet(d, x):
        pl.semaphore_signal(barrier, inc=1, device_id=row_dev(lax.rem(r + d, 16)), device_id_type=MESH)
        pl.semaphore_signal(barrier, inc=1, device_id=col_dev(lax.rem(chip + d, 16)), device_id_type=MESH)
        return x
    lax.fori_loop(1, 16, greet, 0)
    pl.semaphore_signal(barrier, inc=1, device_id=mate, device_id_type=MESH)

    @pl.when(jnp.logical_not(diag))
    def _():
        pl.semaphore_signal(barrier, inc=1, device_id=turned, device_id_type=MESH)

    my_cols = pl.ds(pl.multiple_of(core * 128, 128), 128)
    p_copy.wait()

    def gram_start(x_ref, name, ex):
        gp[...] = mm(x_ref[:, my_cols], x_ref[...], 0, 0)
        ex[r] = rows(gp, chip, 8)[...]

    def gram_send(name, ex):
        spread(name, r, row_dev, lambda k: ex.at[r], ex.at[r], ex.at[0:15])

    def gram_sum(name, ex, g):
        got(ex.at[0:15], name)
        mine = rows(g.at[core], chip, 8)
        mine[...] = total(ex)
        spread(name + "c", chip, col_dev, lambda k: mine, mine, g.at[0, 0:120])

    def gram_finish(name, g):
        got(g.at[0, 0:120], name + "c")
        one(g.at[core], g.at[core], "m_" + name, mate)

    def gram_place(name, g):
        got(g.at[other], "m_" + name)
        a[0:128, :] = g[0]
        a[128:256, :] = g[1]

    gram_start(p_ref, "g1", ex1)
    pl.semaphore_wait(barrier, 32 - diag.astype(jnp.int32))
    gram_send("g1", ex1)

    slab = pl.ds(pl.multiple_of(core * 384 + chip * 24, 8), 24)

    def piece():
        return rcopy(p_ref.at[slab, :], pcs, "tr", turned)

    def top(k):
        return rcopy(p_ref.at[pl.ds(pl.multiple_of(k * 16, 16), 16), my_cols], pts, "top", row_dev(k))

    @pl.when(diag)
    def _():
        pcs[...] = p_ref[slab, :]

    @pl.when(jnp.logical_not(diag))
    def _():
        piece().start()

    @pl.when(r == 0)
    def _():
        def step(k, x):
            top(k).start()
            return x
        lax.fori_loop(1, 16, step, 0)
        pts[...] = p_ref[0:16, my_cols]

    def scattered():
        @pl.when(jnp.logical_not(diag))
        def _():
            piece().wait_send()

        @pl.when(r == 0)
        def _():
            rcopy(p_ref.at[0:240, 0:128], p_ref.at[0:240, 0:128], "top", mate).wait_send()
    done.append(scattered)

    gram_sum("g1", ex1, g1)
    gram_finish("g1", g1)

    @pl.when(jnp.logical_not(diag))
    def _():
        piece().wait_recv()
    pc_mine = rows(pc, r, 24)
    pc_mine[...] = pcs[...]
    spread("pc", r, row_dev, lambda k: pcs, pc_mine, pc.at[0:360])
    gram_place("g1", g1)
    chol_inv(a, w, u1, l1, 64)

    half[...] = mm(p_ref[...], l1[...], 1, 1)
    gram_start(half, "g2", ex2)
    gram_send("g2", ex2)
    got(pc.at[0:360], "pc")
    vc[...] = mm(pc[...], l1[...], 1, 1)
    gram_sum("g2", ex2, g2)
    gram_finish("g2", g2)

    @pl.when(r != 0)
    def _():
        top(0).wait_recv()
    top_mine = rows(pt.at[core], r, 16)
    top_mine[...] = pts[...]
    spread("topg", r, row_dev, lambda k: pts, top_mine, pt.at[0, 0:240])
    gram_place("g2", g2)
    chol_inv(a, w, u2, l2, 64)

    grow = lax.broadcasted_iota(jnp.int32, (N, N), 0)
    gcol = lax.broadcasted_iota(jnp.int32, (N, N), 1)
    ident = jnp.where(grow == gcol, 1.0, 0.0).astype(jnp.float32)
    vc[...] = mm(vc[...], l2[...], 1, 1)

    @pl.when(c == 0)
    def _():
        vc[0:N, :] += ident
    h_copy.wait()

    theirs = pl.multiple_of(other * 384, 384)
    ours = pl.multiple_of(core * 384, 384)
    mbuf[...] = mm(hbuf[pl.ds(theirs, 384), :], vc[...], 1, 0)
    one(mbuf.at[0:192], mrecv.at[0:192], "m_h0", mate)
    one(mbuf.at[192:384], mrecv.at[192:384], "m_h1", mate)
    obuf[...] = mm(hbuf[pl.ds(ours, 384), :], vc[...], 1, 0)
    vr[...] = mm(half[...], l2[...], 1, 1)

    @pl.when(r == 0)
    def _():
        vr[0:N, :] += ident
    got(mrecv.at[0:192], "m_h0")
    obuf[0:192, :] += mrecv[0:192, :]
    got(mrecv.at[192:384], "m_h1")
    obuf[192:384, :] += mrecv[192:384, :]

    sv = mm(vr[pl.ds(ours, 384), :], obuf[...], 0, 0)
    sbuf[0] = sv[0:128, :]
    sbuf[1] = sv[128:256, :]

    def s_piece(k):
        return sbuf.at[:, pl.ds(pl.multiple_of(k * 8, 8), 8), :]
    srs[r] = s_piece(r)[...]
    spread("s", r, row_dev, s_piece, srs.at[r], srs.at[0:15])
    crs[chip] = rows(obuf, chip, 24)[...]
    spread("hr", chip, col_dev, lambda k: rows(obuf, k, 24), crs.at[chip], crs.at[0:15])
    cbuf[...] = mm(hbuf[...], vr[...], 0, 0)
    rrs[r] = rows(cbuf, r, 24)[...]
    spread("hc", r, row_dev, lambda k: rows(cbuf, k, 24), rrs.at[r], rrs.at[0:15])

    got(pt.at[0, 0:240], "topg")
    one(pt.at[core], pt.at[core], "m_top", mate)
    got(pt.at[other], "m_top")
    a[...] = mm(jnp.concatenate([pt[0], pt[1]], axis=1), l1[...], 1, 1)
    a[...] = mm(a[...], l2[...], 1, 1) + ident
    gj_init(w)
    gj_inv(a, w, 0, 32)
    gj_inv(a, w, 32, 32)
    gj_inv(a, w, 64, 32)

    got(srs.at[0:15], "s")
    s1[...] = total(srs)
    one(s1.at[other], smate, "m_s", mate)
    gj_inv(a, w, 96, 32)
    got(smate, "m_s")
    scx[chip] = s1[core] + smate[...]
    spread("sx", chip, col_dev, lambda k: scx.at[chip], scx.at[chip], scx.at[0:15])
    gj_inv(a, w, 128, 32)
    gj_inv(a, w, 160, 32)

    own = hvr.at[pl.ds(ours, 384), :]
    got(crs.at[0:15], "hr")
    hr_mine = rows(own, chip, 24)
    hr_mine[...] = total(crs)
    spread("hrg", chip, col_dev, lambda k: hr_mine, hr_mine, hvr.at[0:360])
    got(scx.at[0:15], "sx")
    s_mine = rows(sfull.at[core], r, 8)
    s_mine[...] = total(scx)
    spread("sg", r, row_dev, lambda k: s_mine, s_mine, sfull.at[0, 0:120])
    got(rrs.at[0:15], "hc")
    hc_mine = rows(hvc, r, 24)
    hc_mine[...] = total(rrs)
    spread("hcg", r, row_dev, lambda k: hc_mine, hc_mine, hvc.at[0:360])
    gj_inv(a, w, 192, 32)
    gj_inv(a, w, 224, 32)
    vr[...] = mm(vr[...], w[...], 1, 0)
    vc[...] = mm(vc[...], w[...], 1, 0)
    got(sfull.at[0, 0:120], "sg")
    one(sfull.at[core], sfull.at[core], "m_sg", mate)
    got(hvr.at[0:360], "hrg")
    one(own, own, "m_hg", mate)
    got(sfull.at[other], "m_sg")
    sv = mm(sfull[0], vc[...], 1, 1)
    sw = mm(sfull[1], vc[...], 1, 1)
    hbuf[...] += mm(vr[:, 0:128], sv, 1, 0) + mm(vr[:, 128:256], sw, 1, 0)
    got(hvr.at[pl.ds(theirs, 384), :], "m_hg")
    hbuf[...] -= mm(hvr[...], vc[...], 1, 1)
    got(hvc.at[0:360], "hcg")
    out_ref[...] = hbuf[...] - mm(vr[...], hvc[...], 1, 1)
    band_ref[...] = -mm(u2[...], u1[...], 1, 0)

    for f in done:
        f()


def shards(hamiltonian, panel):
    vm = pl.BlockSpec(memory_space=pltpu.VMEM)
    hbm = pl.BlockSpec(memory_space=pl.ANY)
    f32 = lambda *s: pltpu.VMEM(s, jnp.float32)
    sq = f32(N, N)
    two = f32(2, 128, N)
    scratch = [f32(768, N), f32(768, 384), f32(128, N), f32(16, 8, N), f32(16, 8, N), two, two,
               f32(16, 128), f32(2, N, 128), f32(24, N), f32(384, N),
               f32(768, N), f32(768, N), f32(384, N), sq, sq, sq, sq, sq, sq,
               f32(384, N), f32(384, N), f32(384, N), f32(384, N), f32(16, 24, N), f32(16, 24, N),
               f32(768, N), f32(384, N),
               two, f32(16, 2, 8, N), f32(2, 8, N), f32(8, N), f32(16, 8, N), two,
               pltpu.SemaphoreType.DMA, pltpu.SemaphoreType.DMA,
               pltpu.SemaphoreType.DMA((len(PHASES),)), pltpu.SemaphoreType.DMA((len(PHASES),))]
    return pl.pallas_call(
        kernel,
        out_shape=[jax.ShapeDtypeStruct((768, 384), jnp.float32), jax.ShapeDtypeStruct((N, N), jnp.float32)],
        in_specs=[hbm, hbm],
        out_specs=[vm, vm],
        scratch_shapes=scratch,
        compiler_params=pltpu.CompilerParams(collective_id=0, has_side_effects=True, vmem_limit_bytes=62 * 2**20),
        cost_estimate=pl.CostEstimate(flops=3 * 10**9, bytes_accessed=4 * 10**6, transcendentals=0),
    )(panel, hamiltonian)


def solution(mesh):
    in_specs = (P("row", "col"), P("row", None))
    out_specs = (P("row", "col"), P())
    return jax.shard_map(shards, mesh=mesh, in_specs=in_specs, out_specs=out_specs, check_vma=False)
```

```python
import functools

import jax
import jax.numpy as jnp
from jax import lax
from jax.experimental import pallas as pl
from jax.experimental.pallas import tpu as pltpu
from jax.sharding import PartitionSpec as P

HI = lax.Precision.HIGHEST
MESH = pl.DeviceIdType.MESH
N = 256


def mm(a, b, ca, cb):
    return lax.dot_general(a, b, (((ca,), (cb,)), ((), ())), precision=HI, preferred_element_type=jnp.float32)

def spread(x, i, rows):
    return jnp.broadcast_to(x[i:i+1, :], (rows, 128))

def stack(parts):
    parts = [p for p in parts if p.shape[0]]
    return parts[0] if len(parts) == 1 else jnp.concatenate(parts, axis=0)

def halves(o):
    return ([0, 1] if o < 128 else [1]), ([0] if o < 128 else [0, 1])

def chol_inv(a, w, u, li, B, after=()):
    row = lax.broadcasted_iota(jnp.int32, (N, N), 0)
    col = lax.broadcasted_iota(jnp.int32, (N, N), 1)
    w[...] = jnp.where(row == col, 1.0, 0.0).astype(jnp.float32)
    sub = lax.broadcasted_iota(jnp.int32, (8, 128), 0)
    for o in range(0, N, B):
        ha, hw = halves(o)
        X = [a[o:o+B, 128*h:128*h+128] for h in ha] + [w[o:o+B, 128*h:128*h+128] for h in hw]
        for q in range(0, B, 8):
            k0 = o + q
            R = B - q
            base = X[ha.index(k0 // 128)]
            l0 = k0 % 128
            C = [jnp.broadcast_to(base[:, l0+k:l0+k+1], (R, 128)) for k in range(8)]
            scale = jnp.ones((8, 128), jnp.float32)
            for i in range(0, 8, 2):
                pa, pb, pd = C[i][i:i+1, :], C[i][i+1:i+2, :], C[i+1][i+1:i+2, :]
                pa, pb, pd = [jnp.broadcast_to(p, (8, 128)) for p in (pa, pb, pd)]
                det = pa*pd - pb*pb
                ra = 1.0 / pa
                rdet = 1.0 / det
                scale = jnp.where(sub == i, lax.rsqrt(pa), jnp.where(sub == i+1, lax.rsqrt(det*ra), scale))
                full = lambda p: jnp.concatenate([p]*(R//8), axis=0) if R > 8 else p
                fa, fb, fra, frd = full(pa), full(pb), full(ra), full(rdet)
                m2 = (C[i+1]*fa - C[i]*fb)*frd
                m1 = (C[i] - m2*fb)*fra
                m2 = stack([jnp.where(sub > i+1, m2[:8], 0.0), m2[8:]])
                m1 = stack([jnp.where(sub > i+1, m1[:8], jnp.where(sub == i+1, pb*ra, 0.0)), m1[8:]])
                for k in range(i+2, 8):
                    C[k] = (C[k] - m1*spread(C[k], i, R)) - m2*spread(C[k], i+1, R)
                X = [(x - m1*spread(x, i, R)) - m2*spread(x, i+1, R) for x in X]
            top = [x[:8]*scale for x in X]
            X = [x[8:] for x in X]
            for j, h in enumerate(ha):
                u[k0:k0+8, 128*h:128*h+128] = top[j]
            for j, h in enumerate(hw):
                li[k0:k0+8, 128*h:128*h+128] = top[len(ha)+j]
            if ha == [1]:
                u[k0:k0+8, 0:128] = jnp.zeros((8, 128), jnp.float32)
            if hw == [0]:
                li[k0:k0+8, 128:256] = jnp.zeros((8, 128), jnp.float32)
        e = o + B
        for at, then in after:
            if at == e:
                then()
        if e < N:
            a0 = 128 * (e // 128)
            lw = 128 if e <= 128 else 256
            for (m0, m1) in ((e, e+B), (e+B, N)):
                if m0 >= m1: continue
                lhs = u[o:e, :][:, m0:m1]
                a[m0:m1, a0:N] -= mm(lhs, u[o:e, a0:N], 0, 0)
                w[m0:m1, 0:lw] -= mm(lhs, li[o:e, 0:lw], 0, 0)
    u[...] = jnp.where(row <= col, u[...], 0.0)

def gj_init(w):
    row = lax.broadcasted_iota(jnp.int32, (N, N), 0)
    col = lax.broadcasted_iota(jnp.int32, (N, N), 1)
    w[...] = jnp.where(row == col, 1.0, 0.0).astype(jnp.float32)

def gj_inv(a, w, o, B):
    sub = lax.broadcasted_iota(jnp.int32, (8, 128), 0)
    ha, hw = halves(o)
    X = [a[o:o+B, 128*h:128*h+128] for h in ha] + [w[o:o+B, 128*h:128*h+128] for h in hw]
    scales = []
    for q in range(0, B, 8):
        k0 = o + q
        base = X[ha.index(k0 // 128)]
        l0 = k0 % 128
        C = [jnp.broadcast_to(base[:, l0+k:l0+k+1], (B, 128)) for k in range(8)]
        scale = jnp.ones((8, 128), jnp.float32)
        for i in range(8):
            p = jnp.broadcast_to(C[i][q+i:q+i+1, :], (8, 128))
            r = 1.0 / p
            scale = jnp.where(sub == i, r, scale)
            m = C[i] * (jnp.concatenate([r]*(B//8), axis=0) if B > 8 else r)
            m = stack([m[:q], jnp.where(sub == i, 0.0, m[q:q+8]), m[q+8:]])
            for k in range(i+1, 8):
                C[k] = C[k] - m*spread(C[k], q+i, B)
            X = [x - m*spread(x, q+i, B) for x in X]
        scales.append(scale)
    scale = jnp.concatenate(scales, axis=0)
    X = [x*scale for x in X]
    for j, h in enumerate(ha):
        a[o:o+B, 128*h:128*h+128] = X[j]
    for j, h in enumerate(hw):
        w[o:o+B, 128*h:128*h+128] = X[len(ha)+j]
    e = o + B
    a0 = 128 * (e // 128)
    lw = 128 if e <= 128 else 256
    h = o // 128
    for (m0, m1) in ((0, o), (e, N)):
        if m0 >= m1: continue
        lhs = a[m0:m1, 128*h:128*h+128][:, o-128*h:e-128*h]
        if a0 < N:
            a[m0:m1, a0:N] -= mm(lhs, a[o:e, a0:N], 1, 0)
        w[m0:m1, 0:lw] -= mm(lhs, w[o:e, 0:lw], 1, 0)

PHASES = ("g1", "g1c", "tr", "top", "pc", "topg", "g2", "g2c", "s", "sx", "sg", "hr", "hc", "hrg", "hcg",
          "m_g1", "m_g2", "m_top", "m_h0", "m_h1", "m_s", "m_sg", "m_hg",
          "he", "hea", "heb", "ht", "m_ht", "sb", "m_b", "sxb", "htx", "htg")


def kernel(p_any, h_any, out_ref, band_ref, p_ref, hbuf, gp, ex1, ex2, g1, g2, pts, pt, pcs, pc,
           half, vr, vc, a, w, u1, l1, u2, l2, mbuf, mrecv, obuf, crs, hha, hhb, hvr, hvc,
           sbuf, srs, s1, smate, scx, sfull, bbuf, brs, b1, bmate, sxb, he, hea, heb, ht2, htt, htq, p_sem, h_sem, send, recv):
    r = lax.axis_index("row")
    c = lax.axis_index("col")
    core = lax.rem(c, 2)
    chip = lax.div(c, 2)
    other = 1 - core
    mate = (r, 2 * chip + other)
    turned = (chip, 2 * r + core)
    diag = chip == r
    done = []

    def rcopy(src, dst, name, dev):
        i = PHASES.index(name)
        return pltpu.make_async_remote_copy(src_ref=src, dst_ref=dst, send_sem=send.at[i], recv_sem=recv.at[i],
                                            device_id=dev, device_id_type=MESH)

    def when(cond, f):
        if cond is None:
            f()
        else:
            pl.when(cond)(f)

    def one(src, dst, name, dev, cond=None):
        when(cond, lambda: rcopy(src, dst, name, dev).start())
        done.append(lambda: when(cond, lambda: rcopy(src, dst, name, dev).wait_send()))

    def got(dst, name, cond=None):
        when(cond, lambda: rcopy(dst, dst, name, mate).wait_recv())

    def row_dev(k):
        return (k, c)

    def col_dev(k):
        return (r, 2 * k + core)

    def spread(name, me, dev, src, dst, fifteen, cond=None):
        def step(d, x):
            k = lax.rem(me + d, 16)
            rcopy(src(k), dst, name, dev(k)).start()
            return x
        when(cond, lambda: lax.fori_loop(1, 16, step, None))
        done.append(lambda: when(cond, lambda: rcopy(fifteen, fifteen, name, mate).wait_send()))

    def rows(ref, k, n):
        return ref.at[pl.ds(pl.multiple_of(k * n, 8), n), :]

    def total(ref):
        t = ref[0]
        for k in range(1, 16):
            t = t + ref[k]
        return t

    p_copy = pltpu.make_async_copy(p_any, p_ref, p_sem)
    p_copy.start()
    h_copy = pltpu.make_async_copy(h_any, hbuf, h_sem)
    h_copy.start()

    barrier = pltpu.get_barrier_semaphore()

    def greet(d, x):
        pl.semaphore_signal(barrier, inc=1, device_id=row_dev(lax.rem(r + d, 16)), device_id_type=MESH)
        pl.semaphore_signal(barrier, inc=1, device_id=col_dev(lax.rem(chip + d, 16)), device_id_type=MESH)
        return x
    lax.fori_loop(1, 16, greet, 0)
    pl.semaphore_signal(barrier, inc=1, device_id=mate, device_id_type=MESH)

    @pl.when(jnp.logical_not(diag))
    def _():
        pl.semaphore_signal(barrier, inc=1, device_id=turned, device_id_type=MESH)

    my_cols = pl.ds(pl.multiple_of(core * 128, 128), 128)
    p_copy.wait()

    def gram_start(x_ref, name, ex):
        gp[...] = mm(x_ref[:, my_cols], x_ref[...], 0, 0)
        ex[r] = rows(gp, chip, 8)[...]

    def gram_send(name, ex):
        spread(name, r, row_dev, lambda k: ex.at[r], ex.at[r], ex.at[0:15])

    def gram_sum(name, ex, g):
        got(ex.at[0:15], name)
        mine = rows(g.at[core], chip, 8)
        mine[...] = total(ex)
        spread(name + "c", chip, col_dev, lambda k: mine, mine, g.at[0, 0:120])

    def gram_finish(name, g):
        got(g.at[0, 0:120], name + "c")
        one(g.at[core], g.at[core], "m_" + name, mate)

    def gram_place(name, g):
        got(g.at[other], "m_" + name)
        a[0:128, :] = g[0]
        a[128:256, :] = g[1]

    gram_start(p_ref, "g1", ex1)
    pl.semaphore_wait(barrier, 32 - diag.astype(jnp.int32))
    gram_send("g1", ex1)

    slab = pl.ds(pl.multiple_of(core * 384 + chip * 24, 8), 24)

    def piece():
        return rcopy(p_ref.at[slab, :], pcs, "tr", turned)

    def top(k):
        return rcopy(p_ref.at[pl.ds(pl.multiple_of(k * 16, 16), 16), my_cols], pts, "top", row_dev(k))

    @pl.when(diag)
    def _():
        pcs[...] = p_ref[slab, :]

    @pl.when(jnp.logical_not(diag))
    def _():
        piece().start()

    @pl.when(r == 0)
    def _():
        def step(k, x):
            top(k).start()
            return x
        lax.fori_loop(1, 16, step, 0)
        pts[...] = p_ref[0:16, my_cols]

    def scattered():
        @pl.when(jnp.logical_not(diag))
        def _():
            piece().wait_send()

        @pl.when(r == 0)
        def _():
            rcopy(p_ref.at[0:240, 0:128], p_ref.at[0:240, 0:128], "top", mate).wait_send()
    done.append(scattered)

    first, lead_chip = c == 0, chip == 0
    h_copy.wait()

    @pl.when(first)
    def _():
        he[...] = hbuf[0:384, 0:N]
    ht_root = jnp.logical_and(first, r == 0)

    @pl.when(ht_root)
    def _():
        ht2[0] = hbuf[0:8, 0:N]
        ht2[1] = hbuf[128:136, 0:N]
    one(hbuf.at[384:768, 0:N], he, "he", mate, first)
    hbuf_sent = [done.pop()]

    def ht_send(k, x):
        for q in range(2):
            rcopy(hbuf.at[pl.ds(pl.multiple_of(q * 128 + k * 8, 8), 8), 0:N], ht2.at[q], "ht", row_dev(k)).start()
        return x
    when(ht_root, lambda: lax.fori_loop(1, 16, ht_send, None))
    hbuf_sent.append(lambda: when(ht_root, lambda: rcopy(hbuf.at[0:240, 0:N], hbuf.at[0:240, 0:N], "ht", mate).wait_send()))

    gram_sum("g1", ex1, g1)

    @pl.when(r != 0)
    def _():
        top(0).wait_recv()
    top_mine = rows(pt.at[core], r, 16)
    top_mine[...] = pts[...]
    spread("topg", r, row_dev, lambda k: pts, top_mine, pt.at[0, 0:240])
    got(he, "he", c == 1)

    @pl.when(lead_chip)
    def _():
        hea[...] = he[0:24, :]
    spread("hea", chip, col_dev, lambda k: rows(he, k, 24), hea, he.at[0:360], lead_chip)
    gram_finish("g1", g1)

    @pl.when(jnp.logical_not(diag))
    def _():
        piece().wait_recv()
    pc_mine = rows(pc, r, 24)
    pc_mine[...] = pcs[...]
    spread("pc", r, row_dev, lambda k: pcs, pc_mine, pc.at[0:360])
    got(hea, "hea", jnp.logical_not(lead_chip))

    @pl.when(diag)
    def _():
        heb[...] = hea[...]
    one(hea, heb, "heb", turned, jnp.logical_not(diag))
    got(ht2, "ht", jnp.logical_and(first, r != 0))

    @pl.when(first)
    def _():
        htt[...] = ht2[0]
    one(ht2.at[1], htt, "m_ht", mate, first)
    gram_place("g1", g1)

    def ht_cross():
        got(htt, "m_ht", c == 1)

        @pl.when(lead_chip)
        def _():
            htq[...] = htt[...]
        spread("htx", chip, col_dev, lambda k: htt, htq, ex1.at[0:15], lead_chip)
    chol_inv(a, w, u1, l1, 64, ((64, ht_cross),))

    half[...] = mm(p_ref[...], l1[...], 1, 1)
    gram_start(half, "g2", ex2)
    gram_send("g2", ex2)
    got(pc.at[0:360], "pc")
    vc[...] = mm(pc[...], l1[...], 1, 1)

    theirs = pl.multiple_of(other * 384, 384)
    ours = pl.multiple_of(core * 384, 384)
    mbuf[...] = mm(hbuf[pl.ds(theirs, 384), :], vc[...], 1, 0)
    one(mbuf.at[0:192], mrecv.at[0:192], "m_h0", mate)
    one(mbuf.at[192:384], mrecv.at[192:384], "m_h1", mate)
    obuf[...] = mm(hbuf[pl.ds(ours, 384), :], vc[...], 1, 0)
    got(mrecv.at[0:192], "m_h0")
    obuf[0:192, :] += mrecv[0:192, :]
    got(mrecv.at[192:384], "m_h1")
    obuf[192:384, :] += mrecv[192:384, :]

    sv = mm(half[pl.ds(ours, 384), :], obuf[...], 0, 0)
    sbuf[0] = sv[0:128, :]
    sbuf[1] = sv[128:256, :]
    one(sbuf.at[other], smate, "m_s", mate)

    @pl.when(lead_chip)
    def _():
        bv = mm(half[pl.ds(ours, 384), :], he[...], 0, 0)
        bbuf[0] = bv[0:128, :]
        bbuf[1] = bv[128:256, :]
    one(bbuf.at[other], bmate, "m_b", mate, lead_chip)
    got(smate, "m_s")
    s1[...] = sbuf[core] + smate[...]
    srs[r] = rows(s1, r, 8)[...]
    spread("s", r, row_dev, lambda k: rows(s1, k, 8), srs.at[r], srs.at[0:15])
    got(bmate, "m_b", lead_chip)

    @pl.when(lead_chip)
    def _():
        b1[...] = bbuf[core] + bmate[...]
        brs[r] = rows(b1, r, 8)[...]
    spread("sb", r, row_dev, lambda k: rows(b1, k, 8), brs.at[r], brs.at[0:15], lead_chip)
    gram_sum("g2", ex2, g2)
    crs[chip] = rows(obuf, chip, 24)[...]
    spread("hr", chip, col_dev, lambda k: rows(obuf, k, 24), crs.at[chip], crs.at[0:15])
    s_early = sfull.at[core, 2, pl.ds(pl.multiple_of(r * 8, 8), 8), :]
    got(htq, "htx", jnp.logical_not(lead_chip))
    s_early[...] = htq[...]
    spread("htg", r, row_dev, lambda k: htq, s_early, sfull.at[0, 2, 0:120])
    gram_finish("g2", g2)
    gram_place("g2", g2)

    def s_cross():
        got(srs.at[0:15], "s")
        scx[chip] = total(srs)
        spread("sx", chip, col_dev, lambda k: scx.at[chip], scx.at[chip], scx.at[0:15])
        got(brs.at[0:15], "sb", lead_chip)

        @pl.when(lead_chip)
        def _():
            sxb[...] = total(brs)
        spread("sxb", chip, col_dev, lambda k: sxb, sxb, scx.at[0:15], lead_chip)

    def turn():
        got(crs.at[0:15], "hr")
        hha[...] = total(crs)

        @pl.when(diag)
        def _():
            hhb[...] = hha[...]
        one(hha, hhb, "hc", turned, jnp.logical_not(diag))

    def top_share():
        got(pt.at[0, 0:240], "topg")
        one(pt.at[core], pt.at[core], "m_top", mate)
    chol_inv(a, w, u2, l2, 64, ((64, s_cross), (128, top_share), (192, turn)))

    grow = lax.broadcasted_iota(jnp.int32, (N, N), 0)
    gcol = lax.broadcasted_iota(jnp.int32, (N, N), 1)
    ident = jnp.where(grow == gcol, 1.0, 0.0).astype(jnp.float32)
    own = hvr.at[pl.ds(ours, 384), :]
    got(scx.at[0:15], "sx")
    got(sxb, "sxb", jnp.logical_not(lead_chip))
    s_mine = sfull.at[core, 0:2, pl.ds(pl.multiple_of(r * 8, 8), 8), :]
    s_mine[0] = total(scx)
    s_mine[1] = sxb[...]
    spread("sg", r, row_dev, lambda k: s_mine, s_mine, sfull.at[0, 0:2, 0:120])
    hr_mine = rows(own, chip, 24)
    hr_mine[...] = mm(hha[...], l2[...], 1, 1) + hea[...]
    spread("hrg", chip, col_dev, lambda k: hr_mine, hr_mine, hvr.at[0:360])
    vr[...] = mm(half[...], l2[...], 1, 1)
    vc[...] = mm(vc[...], l2[...], 1, 1)

    @pl.when(r == 0)
    def _():
        vr[0:N, :] += ident

    @pl.when(c == 0)
    def _():
        vc[0:N, :] += ident

    got(pt.at[other], "m_top")
    a[...] = mm(jnp.concatenate([pt[0], pt[1]], axis=1), l1[...], 1, 1)
    a[...] = mm(a[...], l2[...], 1, 1) + ident
    gj_init(w)
    gj_inv(a, w, 0, 32)
    got(hhb, "hc", jnp.logical_not(diag))
    got(heb, "heb", jnp.logical_not(diag))
    hc_mine = rows(hvc, r, 24)
    hc_mine[...] = mm(hhb[...], l2[...], 1, 1) + heb[...]
    spread("hcg", r, row_dev, lambda k: hc_mine, hc_mine, hvc.at[0:360])
    for o in range(32, N, 32):
        gj_inv(a, w, o, 32)
    vr[...] = mm(vr[...], w[...], 1, 0)
    vc[...] = mm(vc[...], w[...], 1, 0)

    band_ref[...] = -mm(u2[...], u1[...], 1, 0)
    got(sfull.at[0, 2, 0:120], "htg")
    got(sfull.at[0, 0:2, 0:120], "sg")
    one(sfull.at[core], sfull.at[core], "m_sg", mate)
    got(sfull.at[other], "m_sg")
    shh, sb, stt = [jnp.concatenate([sfull[0, i], sfull[1, i]], axis=0) for i in range(3)]
    a[...] = mm(mm(l2[...], shh, 1, 0), l2[...], 1, 1) + mm(l2[...], sb, 1, 0) + mm(sb, l2[...], 0, 1) + stt
    for f in hbuf_sent:
        f()
    hbuf[...] += mm(vr[...], mm(a[...], vc[...], 1, 1), 1, 0)
    got(hvr.at[0:360], "hrg")
    one(own, own, "m_hg", mate)
    got(hvr.at[pl.ds(theirs, 384), :], "m_hg")
    hbuf[...] -= mm(hvr[...], vc[...], 1, 1)
    got(hvc.at[0:360], "hcg")
    out_ref[...] = hbuf[...] - mm(vr[...], hvc[...], 1, 1)

    for f in done:
        f()


def shards(hamiltonian, panel):
    vm = pl.BlockSpec(memory_space=pltpu.VMEM)
    hbm = pl.BlockSpec(memory_space=pltpu.HBM)
    f32 = lambda *s: pltpu.VMEM(s, jnp.float32)
    sq = f32(N, N)
    two = f32(2, 128, N)
    scratch = [f32(768, N), f32(768, 384), f32(128, N), f32(16, 8, N), f32(16, 8, N), two, two,
               f32(16, 128), f32(2, N, 128), f32(24, N), f32(384, N),
               f32(768, N), f32(768, N), f32(384, N), sq, sq, sq, sq, sq, sq,
               f32(384, N), f32(384, N), f32(384, N), f32(16, 24, N), f32(24, N), f32(24, N),
               f32(768, N), f32(384, N),
               two, f32(16, 8, N), f32(128, N), f32(128, N), f32(16, 8, N), f32(2, 3, 128, N),
               two, f32(16, 8, N), f32(128, N), f32(128, N), f32(8, N), f32(384, N), f32(24, N), f32(24, N),
               f32(2, 8, N), f32(8, N), f32(8, N),
               pltpu.SemaphoreType.DMA, pltpu.SemaphoreType.DMA,
               pltpu.SemaphoreType.DMA((len(PHASES),)), pltpu.SemaphoreType.DMA((len(PHASES),))]
    return pl.pallas_call(
        kernel,
        out_shape=[jax.ShapeDtypeStruct((768, 384), jnp.float32), jax.ShapeDtypeStruct((N, N), jnp.float32)],
        in_specs=[hbm, hbm],
        out_specs=[vm, vm],
        scratch_shapes=scratch,
        compiler_params=pltpu.CompilerParams(collective_id=0, has_side_effects=True, vmem_limit_bytes=58 * 2**20),
        cost_estimate=pl.CostEstimate(flops=3 * 10**9, bytes_accessed=4 * 10**6, transcendentals=0),
    )(panel, hamiltonian)


def solution(mesh):
    in_specs = (P("row", "col"), P("row", None))
    out_specs = (P("row", "col"), P())
    return jax.shard_map(shards, mesh=mesh, in_specs=in_specs, out_specs=out_specs, check_vma=False)
```

```python
import functools

import jax
import jax.numpy as jnp
from jax import lax
from jax.experimental import pallas as pl
from jax.experimental.pallas import tpu as pltpu
from jax.sharding import PartitionSpec as P

HI = lax.Precision.HIGHEST
MESH = pl.DeviceIdType.MESH
N = 256


def mm(a, b, ca, cb):
    return lax.dot_general(a, b, (((ca,), (cb,)), ((), ())), precision=HI, preferred_element_type=jnp.float32)

def spread(x, i, rows):
    return jnp.broadcast_to(x[i:i+1, :], (rows, 128))

def stack(parts):
    parts = [p for p in parts if p.shape[0]]
    return parts[0] if len(parts) == 1 else jnp.concatenate(parts, axis=0)

def halves(o):
    return ([0, 1] if o < 128 else [1]), ([0] if o < 128 else [0, 1])

def chol_inv(a, w, u, li, B, after=()):
    row = lax.broadcasted_iota(jnp.int32, (N, N), 0)
    col = lax.broadcasted_iota(jnp.int32, (N, N), 1)
    w[...] = jnp.where(row == col, 1.0, 0.0).astype(jnp.float32)
    sub = lax.broadcasted_iota(jnp.int32, (8, 128), 0)
    for o in range(0, N, B):
        ha, hw = halves(o)
        X = [a[o:o+B, 128*h:128*h+128] for h in ha] + [w[o:o+B, 128*h:128*h+128] for h in hw]
        for q in range(0, B, 8):
            k0 = o + q
            R = B - q
            base = X[ha.index(k0 // 128)]
            l0 = k0 % 128
            C = [jnp.broadcast_to(base[:, l0+k:l0+k+1], (R, 128)) for k in range(8)]
            scale = jnp.ones((8, 128), jnp.float32)
            for i in range(0, 8, 2):
                pa, pb, pd = C[i][i:i+1, :], C[i][i+1:i+2, :], C[i+1][i+1:i+2, :]
                pa, pb, pd = [jnp.broadcast_to(p, (8, 128)) for p in (pa, pb, pd)]
                det = pa*pd - pb*pb
                ra = 1.0 / pa
                rdet = 1.0 / det
                scale = jnp.where(sub == i, lax.rsqrt(pa), jnp.where(sub == i+1, lax.rsqrt(det*ra), scale))
                full = lambda p: jnp.concatenate([p]*(R//8), axis=0) if R > 8 else p
                fa, fb, fra, frd = full(pa), full(pb), full(ra), full(rdet)
                m2 = (C[i+1]*fa - C[i]*fb)*frd
                m1 = (C[i] - m2*fb)*fra
                m2 = stack([jnp.where(sub > i+1, m2[:8], 0.0), m2[8:]])
                m1 = stack([jnp.where(sub > i+1, m1[:8], jnp.where(sub == i+1, pb*ra, 0.0)), m1[8:]])
                for k in range(i+2, 8):
                    C[k] = (C[k] - m1*spread(C[k], i, R)) - m2*spread(C[k], i+1, R)
                X = [(x - m1*spread(x, i, R)) - m2*spread(x, i+1, R) for x in X]
            top = [x[:8]*scale for x in X]
            X = [x[8:] for x in X]
            for j, h in enumerate(ha):
                u[k0:k0+8, 128*h:128*h+128] = top[j]
            for j, h in enumerate(hw):
                li[k0:k0+8, 128*h:128*h+128] = top[len(ha)+j]
            if ha == [1]:
                u[k0:k0+8, 0:128] = jnp.zeros((8, 128), jnp.float32)
            if hw == [0]:
                li[k0:k0+8, 128:256] = jnp.zeros((8, 128), jnp.float32)
        e = o + B
        for at, then in after:
            if at == e:
                then()
        if e < N:
            a0 = 128 * (e // 128)
            lw = 128 if e <= 128 else 256
            for (m0, m1) in ((e, e+B), (e+B, N)):
                if m0 >= m1: continue
                lhs = u[o:e, :][:, m0:m1]
                a[m0:m1, a0:N] -= mm(lhs, u[o:e, a0:N], 0, 0)
                w[m0:m1, 0:lw] -= mm(lhs, li[o:e, 0:lw], 0, 0)
    u[...] = jnp.where(row <= col, u[...], 0.0)

def gj_init(w):
    row = lax.broadcasted_iota(jnp.int32, (N, N), 0)
    col = lax.broadcasted_iota(jnp.int32, (N, N), 1)
    w[...] = jnp.where(row == col, 1.0, 0.0).astype(jnp.float32)

def gj_inv(a, w, o, B):
    sub = lax.broadcasted_iota(jnp.int32, (8, 128), 0)
    ha, hw = halves(o)
    X = [a[o:o+B, 128*h:128*h+128] for h in ha] + [w[o:o+B, 128*h:128*h+128] for h in hw]
    scales = []
    for q in range(0, B, 8):
        k0 = o + q
        base = X[ha.index(k0 // 128)]
        l0 = k0 % 128
        C = [jnp.broadcast_to(base[:, l0+k:l0+k+1], (B, 128)) for k in range(8)]
        scale = jnp.ones((8, 128), jnp.float32)
        for i in range(8):
            p = jnp.broadcast_to(C[i][q+i:q+i+1, :], (8, 128))
            r = 1.0 / p
            scale = jnp.where(sub == i, r, scale)
            m = C[i] * (jnp.concatenate([r]*(B//8), axis=0) if B > 8 else r)
            m = stack([m[:q], jnp.where(sub == i, 0.0, m[q:q+8]), m[q+8:]])
            for k in range(i+1, 8):
                C[k] = C[k] - m*spread(C[k], q+i, B)
            X = [x - m*spread(x, q+i, B) for x in X]
        scales.append(scale)
    scale = jnp.concatenate(scales, axis=0)
    X = [x*scale for x in X]
    for j, h in enumerate(ha):
        a[o:o+B, 128*h:128*h+128] = X[j]
    for j, h in enumerate(hw):
        w[o:o+B, 128*h:128*h+128] = X[len(ha)+j]
    e = o + B
    a0 = 128 * (e // 128)
    lw = 128 if e <= 128 else 256
    h = o // 128
    for (m0, m1) in ((0, o), (e, N)):
        if m0 >= m1: continue
        lhs = a[m0:m1, 128*h:128*h+128][:, o-128*h:e-128*h]
        if a0 < N:
            a[m0:m1, a0:N] -= mm(lhs, a[o:e, a0:N], 1, 0)
        w[m0:m1, 0:lw] -= mm(lhs, w[o:e, 0:lw], 1, 0)

PHASES = ("g1", "g1c", "tr", "top", "pc", "topg", "g2", "g2c", "s", "sx", "sg", "hr", "hc", "hrg", "hcg",
          "m_g1", "m_g2", "m_top", "m_h0", "m_h1", "m_s", "m_sg", "m_hg",
          "he", "hea", "heb", "ht", "m_ht", "sb", "m_b", "sxb", "htx", "htg")


def kernel(p_any, h_any, out_ref, band_ref, p_ref, hbuf, gp, ex1, ex2, g1, g2, pts, pt, pcs, pc,
           half, vr, vc, a, w, u1, l1, u2, l2, mbuf, mrecv, obuf, crs, hha, hhb, hvr, hvc,
           sbuf, srs, s1, smate, scx, sfull, bbuf, brs, b1, bmate, sxb, he, hea, heb, ht2, htt, htq, p_sem, h_sem, send, recv):
    r = lax.axis_index("row")
    c = lax.axis_index("col")
    core = lax.rem(c, 2)
    chip = lax.div(c, 2)
    other = 1 - core
    mate = (r, 2 * chip + other)
    turned = (chip, 2 * r + core)
    diag = chip == r
    done = []

    def rcopy(src, dst, name, dev):
        i = PHASES.index(name)
        return pltpu.make_async_remote_copy(src_ref=src, dst_ref=dst, send_sem=send.at[i], recv_sem=recv.at[i],
                                            device_id=dev, device_id_type=MESH)

    def when(cond, f):
        if cond is None:
            f()
        else:
            pl.when(cond)(f)

    def one(src, dst, name, dev, cond=None):
        when(cond, lambda: rcopy(src, dst, name, dev).start())
        done.append(lambda: when(cond, lambda: rcopy(src, dst, name, dev).wait_send()))

    def got(dst, name, cond=None):
        when(cond, lambda: rcopy(dst, dst, name, mate).wait_recv())

    def row_dev(k):
        return (k, c)

    def col_dev(k):
        return (r, 2 * k + core)

    def spread(name, me, dev, src, dst, fifteen, cond=None):
        def step(d, x):
            k = lax.rem(me + d, 16)
            rcopy(src(k), dst, name, dev(k)).start()
            return x
        when(cond, lambda: lax.fori_loop(1, 16, step, None))
        done.append(lambda: when(cond, lambda: rcopy(fifteen, fifteen, name, mate).wait_send()))

    def rows(ref, k, n):
        return ref.at[pl.ds(pl.multiple_of(k * n, 8), n), :]

    def total(ref):
        t = ref[0]
        for k in range(1, 16):
            t = t + ref[k]
        return t

    p_copy = pltpu.make_async_copy(p_any, p_ref, p_sem)
    p_copy.start()
    h_copy = pltpu.make_async_copy(h_any, hbuf, h_sem)
    h_copy.start()

    barrier = pltpu.get_barrier_semaphore()

    def greet(d, x):
        pl.semaphore_signal(barrier, inc=1, device_id=row_dev(lax.rem(r + d, 16)), device_id_type=MESH)
        pl.semaphore_signal(barrier, inc=1, device_id=col_dev(lax.rem(chip + d, 16)), device_id_type=MESH)
        return x
    lax.fori_loop(1, 16, greet, 0)
    pl.semaphore_signal(barrier, inc=1, device_id=mate, device_id_type=MESH)

    @pl.when(jnp.logical_not(diag))
    def _():
        pl.semaphore_signal(barrier, inc=1, device_id=turned, device_id_type=MESH)

    my_cols = pl.ds(pl.multiple_of(core * 128, 128), 128)
    p_copy.wait()

    def gram_start(x_ref, name, ex):
        gp[...] = mm(x_ref[:, my_cols], x_ref[...], 0, 0)
        ex[r] = rows(gp, chip, 8)[...]

    def gram_send(name, ex):
        spread(name, r, row_dev, lambda k: ex.at[r], ex.at[r], ex.at[0:15])

    def gram_sum(name, ex, g):
        got(ex.at[0:15], name)
        mine = rows(g.at[core], chip, 8)
        mine[...] = total(ex)
        spread(name + "c", chip, col_dev, lambda k: mine, mine, g.at[0, 0:120])

    def gram_finish(name, g):
        got(g.at[0, 0:120], name + "c")
        one(g.at[core], g.at[core], "m_" + name, mate)

    def gram_place(name, g):
        got(g.at[other], "m_" + name)
        a[0:128, :] = g[0]
        a[128:256, :] = g[1]

    gram_start(p_ref, "g1", ex1)
    pl.semaphore_wait(barrier, 32 - diag.astype(jnp.int32))
    gram_send("g1", ex1)

    slab = pl.ds(pl.multiple_of(core * 384 + chip * 24, 8), 24)

    def piece():
        return rcopy(p_ref.at[slab, :], pcs, "tr", turned)

    def top(k):
        return rcopy(p_ref.at[pl.ds(pl.multiple_of(k * 16, 16), 16), my_cols], pts, "top", row_dev(k))

    @pl.when(diag)
    def _():
        pcs[...] = p_ref[slab, :]

    @pl.when(jnp.logical_not(diag))
    def _():
        piece().start()

    @pl.when(r == 0)
    def _():
        def step(k, x):
            top(k).start()
            return x
        lax.fori_loop(1, 16, step, 0)
        pts[...] = p_ref[0:16, my_cols]

    def scattered():
        @pl.when(jnp.logical_not(diag))
        def _():
            piece().wait_send()

        @pl.when(r == 0)
        def _():
            rcopy(p_ref.at[0:240, 0:128], p_ref.at[0:240, 0:128], "top", mate).wait_send()
    done.append(scattered)

    first, lead_chip = c == 0, chip == 0
    h_copy.wait()

    @pl.when(first)
    def _():
        he[...] = hbuf[0:384, 0:N]
    ht_root = jnp.logical_and(first, r == 0)

    @pl.when(ht_root)
    def _():
        ht2[0] = hbuf[0:8, 0:N]
        ht2[1] = hbuf[128:136, 0:N]
    one(hbuf.at[384:768, 0:N], he, "he", mate, first)
    hbuf_sent = [done.pop()]

    def ht_send(k, x):
        for q in range(2):
            rcopy(hbuf.at[pl.ds(pl.multiple_of(q * 128 + k * 8, 8), 8), 0:N], ht2.at[q], "ht", row_dev(k)).start()
        return x
    when(ht_root, lambda: lax.fori_loop(1, 16, ht_send, None))
    hbuf_sent.append(lambda: when(ht_root, lambda: rcopy(hbuf.at[0:240, 0:N], hbuf.at[0:240, 0:N], "ht", mate).wait_send()))

    gram_sum("g1", ex1, g1)

    @pl.when(r != 0)
    def _():
        top(0).wait_recv()
    top_mine = rows(pt.at[core], r, 16)
    top_mine[...] = pts[...]
    spread("topg", r, row_dev, lambda k: pts, top_mine, pt.at[0, 0:240])
    got(he, "he", c == 1)

    @pl.when(lead_chip)
    def _():
        hea[...] = he[0:24, :]
    spread("hea", chip, col_dev, lambda k: rows(he, k, 24), hea, he.at[0:360], lead_chip)
    gram_finish("g1", g1)

    @pl.when(jnp.logical_not(diag))
    def _():
        piece().wait_recv()
    pc_mine = rows(pc, r, 24)
    pc_mine[...] = pcs[...]
    spread("pc", r, row_dev, lambda k: pcs, pc_mine, pc.at[0:360])
    got(hea, "hea", jnp.logical_not(lead_chip))

    @pl.when(diag)
    def _():
        heb[...] = hea[...]
    one(hea, heb, "heb", turned, jnp.logical_not(diag))
    got(ht2, "ht", jnp.logical_and(first, r != 0))

    @pl.when(first)
    def _():
        htt[...] = ht2[0]
    one(ht2.at[1], htt, "m_ht", mate, first)
    gram_place("g1", g1)

    def ht_cross():
        got(htt, "m_ht", c == 1)

        @pl.when(lead_chip)
        def _():
            htq[...] = htt[...]
        spread("htx", chip, col_dev, lambda k: htt, htq, ex1.at[0:15], lead_chip)
    chol_inv(a, w, u1, l1, 64, ((64, ht_cross),))

    half[...] = mm(p_ref[...], l1[...], 1, 1)
    gram_start(half, "g2", ex2)
    gram_send("g2", ex2)
    got(pc.at[0:360], "pc")
    vc[...] = mm(pc[...], l1[...], 1, 1)

    theirs = pl.multiple_of(other * 384, 384)
    ours = pl.multiple_of(core * 384, 384)
    mbuf[...] = mm(hbuf[pl.ds(theirs, 384), :], vc[...], 1, 0)
    one(mbuf.at[0:192], mrecv.at[0:192], "m_h0", mate)
    one(mbuf.at[192:384], mrecv.at[192:384], "m_h1", mate)
    obuf[...] = mm(hbuf[pl.ds(ours, 384), :], vc[...], 1, 0)
    got(mrecv.at[0:192], "m_h0")
    obuf[0:192, :] += mrecv[0:192, :]
    got(mrecv.at[192:384], "m_h1")
    obuf[192:384, :] += mrecv[192:384, :]

    sv = mm(half[pl.ds(ours, 384), :], obuf[...], 0, 0)
    sbuf[0] = sv[0:128, :]
    sbuf[1] = sv[128:256, :]
    one(sbuf.at[other], smate, "m_s", mate)

    @pl.when(lead_chip)
    def _():
        bv = mm(half[pl.ds(ours, 384), :], he[...], 0, 0)
        bbuf[0] = bv[0:128, :]
        bbuf[1] = bv[128:256, :]
    one(bbuf.at[other], bmate, "m_b", mate, lead_chip)
    got(smate, "m_s")
    s1[...] = sbuf[core] + smate[...]
    srs[r] = rows(s1, r, 8)[...]
    spread("s", r, row_dev, lambda k: rows(s1, k, 8), srs.at[r], srs.at[0:15])
    got(bmate, "m_b", lead_chip)

    @pl.when(lead_chip)
    def _():
        b1[...] = bbuf[core] + bmate[...]
        brs[r] = rows(b1, r, 8)[...]
    spread("sb", r, row_dev, lambda k: rows(b1, k, 8), brs.at[r], brs.at[0:15], lead_chip)
    gram_sum("g2", ex2, g2)
    crs[chip] = rows(obuf, chip, 24)[...]
    spread("hr", chip, col_dev, lambda k: rows(obuf, k, 24), crs.at[chip], crs.at[0:15])
    s_early = sfull.at[core, 2, pl.ds(pl.multiple_of(r * 8, 8), 8), :]
    got(htq, "htx", jnp.logical_not(lead_chip))
    s_early[...] = htq[...]
    spread("htg", r, row_dev, lambda k: htq, s_early, sfull.at[0, 2, 0:120])
    gram_finish("g2", g2)
    gram_place("g2", g2)

    def s_cross():
        got(srs.at[0:15], "s")
        scx[chip] = total(srs)
        spread("sx", chip, col_dev, lambda k: scx.at[chip], scx.at[chip], scx.at[0:15])
        got(brs.at[0:15], "sb", lead_chip)

        @pl.when(lead_chip)
        def _():
            sxb[...] = total(brs)
        spread("sxb", chip, col_dev, lambda k: sxb, sxb, scx.at[0:15], lead_chip)

    def turn():
        got(crs.at[0:15], "hr")
        hha[...] = total(crs)

        @pl.when(diag)
        def _():
            hhb[...] = hha[...]
        one(hha, hhb, "hc", turned, jnp.logical_not(diag))

    def top_share():
        got(pt.at[0, 0:240], "topg")
        one(pt.at[core], pt.at[core], "m_top", mate)
    chol_inv(a, w, u2, l2, 64, ((64, s_cross), (128, top_share), (192, turn)))

    grow = lax.broadcasted_iota(jnp.int32, (N, N), 0)
    gcol = lax.broadcasted_iota(jnp.int32, (N, N), 1)
    ident = jnp.where(grow == gcol, 1.0, 0.0).astype(jnp.float32)
    own = hvr.at[pl.ds(ours, 384), :]
    got(scx.at[0:15], "sx")
    got(sxb, "sxb", jnp.logical_not(lead_chip))
    s_mine = sfull.at[core, 0:2, pl.ds(pl.multiple_of(r * 8, 8), 8), :]
    s_mine[0] = total(scx)
    s_mine[1] = sxb[...]
    spread("sg", r, row_dev, lambda k: s_mine, s_mine, sfull.at[0, 0:2, 0:120])
    hr_mine = rows(own, chip, 24)
    hr_mine[...] = mm(hha[...], l2[...], 1, 1) + hea[...]
    spread("hrg", chip, col_dev, lambda k: hr_mine, hr_mine, hvr.at[0:360])
    got(pt.at[other], "m_top")
    a[...] = mm(jnp.concatenate([pt[0], pt[1]], axis=1), l1[...], 1, 1)
    a[...] = mm(a[...], l2[...], 1, 1) + ident
    gj_init(w)
    gj_inv(a, w, 0, 32)
    got(hhb, "hc", jnp.logical_not(diag))
    got(heb, "heb", jnp.logical_not(diag))
    hc_mine = rows(hvc, r, 24)
    hc_mine[...] = mm(hhb[...], l2[...], 1, 1) + heb[...]
    spread("hcg", r, row_dev, lambda k: hc_mine, hc_mine, hvc.at[0:360])
    for o in range(32, N, 32):
        gj_inv(a, w, o, 32)
    a[...] = mm(l2[...], w[...], 0, 0)
    vr[...] = mm(half[...], a[...], 1, 0)
    vc[...] = mm(vc[...], a[...], 1, 0)

    @pl.when(r == 0)
    def _():
        vr[0:N, :] += w[...]

    @pl.when(c == 0)
    def _():
        vc[0:N, :] += w[...]

    band_ref[...] = -mm(u2[...], u1[...], 1, 0)
    got(sfull.at[0, 2, 0:120], "htg")
    got(sfull.at[0, 0:2, 0:120], "sg")
    one(sfull.at[core], sfull.at[core], "m_sg", mate)
    got(sfull.at[other], "m_sg")
    shh, sb, stt = [jnp.concatenate([sfull[0, i], sfull[1, i]], axis=0) for i in range(3)]
    a[...] = mm(mm(l2[...], shh, 1, 0), l2[...], 1, 1) + mm(l2[...], sb, 1, 0) + mm(sb, l2[...], 0, 1) + stt
    for f in hbuf_sent:
        f()
    hbuf[...] += mm(vr[...], mm(a[...], vc[...], 1, 1), 1, 0)
    got(hvr.at[0:360], "hrg")
    one(own, own, "m_hg", mate)
    got(hvr.at[pl.ds(theirs, 384), :], "m_hg")
    hbuf[...] -= mm(hvr[...], vc[...], 1, 1)
    got(hvc.at[0:360], "hcg")
    out_ref[...] = hbuf[...] - mm(vr[...], hvc[...], 1, 1)

    for f in done:
        f()


def shards(hamiltonian, panel):
    vm = pl.BlockSpec(memory_space=pltpu.VMEM)
    hbm = pl.BlockSpec(memory_space=pltpu.HBM)
    f32 = lambda *s: pltpu.VMEM(s, jnp.float32)
    sq = f32(N, N)
    two = f32(2, 128, N)
    scratch = [f32(768, N), f32(768, 384), f32(128, N), f32(16, 8, N), f32(16, 8, N), two, two,
               f32(16, 128), f32(2, N, 128), f32(24, N), f32(384, N),
               f32(768, N), f32(768, N), f32(384, N), sq, sq, sq, sq, sq, sq,
               f32(384, N), f32(384, N), f32(384, N), f32(16, 24, N), f32(24, N), f32(24, N),
               f32(768, N), f32(384, N),
               two, f32(16, 8, N), f32(128, N), f32(128, N), f32(16, 8, N), f32(2, 3, 128, N),
               two, f32(16, 8, N), f32(128, N), f32(128, N), f32(8, N), f32(384, N), f32(24, N), f32(24, N),
               f32(2, 8, N), f32(8, N), f32(8, N),
               pltpu.SemaphoreType.DMA, pltpu.SemaphoreType.DMA,
               pltpu.SemaphoreType.DMA((len(PHASES),)), pltpu.SemaphoreType.DMA((len(PHASES),))]
    return pl.pallas_call(
        kernel,
        out_shape=[jax.ShapeDtypeStruct((768, 384), jnp.float32), jax.ShapeDtypeStruct((N, N), jnp.float32)],
        in_specs=[hbm, hbm],
        out_specs=[vm, vm],
        scratch_shapes=scratch,
        compiler_params=pltpu.CompilerParams(collective_id=0, has_side_effects=True, vmem_limit_bytes=58 * 2**20),
        cost_estimate=pl.CostEstimate(flops=3 * 10**9, bytes_accessed=4 * 10**6, transcendentals=0),
    )(panel, hamiltonian)


def solution(mesh):
    in_specs = (P("row", "col"), P("row", None))
    out_specs = (P("row", "col"), P())
    return jax.shard_map(shards, mesh=mesh, in_specs=in_specs, out_specs=out_specs, check_vma=False)
```
